32 devices in a mesh: groups: 2 (over y), sec: 4 (over z), grid: 4 (over x, core).
Axes of the slice: x: 2, y: 2, z: 4, core: 2. Of those that a mesh axis runs over, the one named last changes fastest.
Arguments:
- modes: bfloat16 [8, 4096, 1024], P(('groups', 'sec'), 'grid'), parts along dimension 0
- exit_modes: bfloat16 [8192, 1024], P(('groups', 'grid')), parts along dimension 0
- pattern: int32 [8, 8, 2], P(('groups', 'sec')), parts along dimension 0, may hold values 0 or 1
- attenuation: float32 [8, 1024], P(('groups', 'sec')), parts along dimension 0, may hold values from 0.96 to 1
- reflection: float32 [8, 1024], P(('groups', 'sec')), parts along dimension 0, may hold values from -0.15 to 0.15
Outputs:
- cascade: float32 [6, 8, 128, 128], P('groups', 'grid', 'sec'), parts along dimension 0
The draws below stay inside these ranges and needn't reach their ends.
There are 2 independent parts, one for each index of `groups`. The reference program is written for one: setup_inputs(seed, part) draws one part's arguments, and reference() takes and returns one part's arrays. A program takes and returns all parts, laid end to end along the dimension named above; each array names one. Nothing has to cross between parts.
All inputs are finite; a program needn't handle non-finite values. No bound on the sum of `pattern` on one device may be relied on, other than what follows from the above.
Results may differ from the reference program's by a relative error of at most 0.0003.
Values may be sent and summed in bfloat16 or wider, within the bound.
No kernel may reach another device: no remote copies, remote signals or barrier semaphores. Data moves between devices by JAX's collectives and lax.ppermute only.
A program may use at most 64 MiB of HBM per device.

```python
import math
import jax
import jax.numpy as jnp
from jax import lax

KC = 8
CW = 128
SEC_DEV = 1
M = 1024
NS = 4
GRID = 4096


def mode_basis():
    points = jnp.arange(GRID, dtype=jnp.float32)[:, None]
    orders = jnp.arange(M, dtype=jnp.float32)[None, :]
    weights = jnp.where(orders == 0, math.sqrt(1.0 / GRID), math.sqrt(2.0 / GRID))
    return weights * jnp.cos(math.pi * (points + 0.5) * orders / GRID)


def perturbed(key, shape):
    jitter = jax.random.normal(key, shape, jnp.float32)
    return jitter * (0.4 / math.sqrt(GRID))


def draw_modes(key, part):
    basis = mode_basis()
    return (basis[None] + perturbed(jax.random.fold_in(key, 11), (NS, GRID, M))).astype(jnp.bfloat16)


def draw_exit_modes(key, part):
    basis = mode_basis()
    return (basis + perturbed(jax.random.fold_in(key, 23), (GRID, M))).astype(jnp.bfloat16)


def set_ends(drawn, key, least, largest):
    spot = [jax.random.randint(jax.random.fold_in(key, axis), (), 0, length) for axis, length in enumerate(drawn.shape)]
    longest = drawn.shape.index(max(drawn.shape))
    neighbour = spot[:longest] + [(spot[longest] + 1) % drawn.shape[longest]] + spot[longest + 1:]
    return drawn.at[tuple(spot)].set(least).at[tuple(neighbour)].set(largest)


def levels(rng, extent, split, low, top_value):
    factor_of, own = 1.0, jax.random.fold_in(rng, 6)
    for dim, blocks in split:
        heights = jnp.exp(jax.random.uniform(jax.random.fold_in(own, dim), (blocks,), jnp.float32, low / len(split), top_value / len(split)))
        factor_of = factor_of * jnp.repeat(heights, extent[dim] // blocks).reshape([-1 if axis == dim else 1 for axis in range(len(extent))])
    return factor_of


def setup_inputs(seed: int = 0, part: int = 0) -> dict:
    key_list = jax.random.split(jax.random.key(seed), 6)
    part_keys = jax.random.split(jax.random.fold_in(key_list[5], part), 6)
    return {
        "modes": draw_modes(jax.random.fold_in(jax.random.fold_in(key_list[5], part), 71), part),
        "exit_modes": draw_exit_modes(jax.random.fold_in(jax.random.fold_in(key_list[5], part), 71), part),
        "pattern": set_ends((jax.random.randint(part_keys[2], (NS, KC, 2), 0, 2) < 1).astype(jnp.int32), jax.random.fold_in(part_keys[2], 1), 0, 1),
        "attenuation": jnp.clip(jnp.exp(math.log(1.0) - 0.040822017 * jax.random.uniform(part_keys[3], (NS, M), jnp.float32) ** levels(part_keys[3], (NS, M), ((0, 4),), -0.2, 0.2)), 0.96, 1.0),
        "reflection": jnp.clip(jax.random.uniform(part_keys[4], (NS, M), jnp.float32, -0.15, 0.15) * levels(part_keys[4], (NS, M), ((0, 4),), -0.4, 0.0), -0.15, 0.15),
    }


def batch_mul(left_side, right_side):
    return jnp.einsum('kij,kjl->kil', left_side, right_side, precision=lax.Precision.HIGHEST)

def flipped(matrix):
    return jnp.swapaxes(matrix, 1, 2)

def star_product(first, second):
    trans_a, front_a, back_a = (first[0], first[1], first[2])
    trans_b, front_b, back_b = (second[0], second[1], second[2])
    bounce = batch_mul(back_a, front_b)
    bounce_sq = batch_mul(bounce, bounce)
    inner = trans_a + batch_mul(bounce, trans_a)
    inner = inner + batch_mul(bounce_sq, inner)
    trans_new = batch_mul(trans_b, inner)
    front_new = front_a + batch_mul(flipped(trans_a), batch_mul(front_b, inner))
    reverse_b = flipped(trans_b)
    behind = reverse_b + batch_mul(flipped(bounce), reverse_b)
    behind = behind + batch_mul(flipped(bounce_sq), behind)
    back_new = back_b + batch_mul(trans_b, batch_mul(back_a, behind))
    return jnp.stack([trans_new, front_new, back_new])

def tile_mask(flags, width):
    tiles = jnp.arange(width) // (width // 2)
    upper = (tiles[:, None] < tiles[None, :]).astype(jnp.float32)
    lower = (tiles[:, None] > tiles[None, :]).astype(jnp.float32)
    flag_up = flags[:, 0].astype(jnp.float32)[:, None, None]
    flag_low = flags[:, 1].astype(jnp.float32)[:, None, None]
    return 1.0 - upper - lower + upper * flag_up + lower * flag_low

def unit_matrices(intersection, decay_now, mirror):
    passing = jnp.sqrt(1.0 - mirror * mirror)
    trans_unit = passing[:, :, None] * intersection * decay_now[:, None, :]
    ident = jnp.eye(intersection.shape[1], dtype=jnp.float32)
    front_unit = ident[None] * (decay_now * decay_now * mirror)[:, :, None]
    back_unit = -ident[None] * mirror[:, :, None]
    return jnp.stack([trans_unit, front_unit, back_unit])

def intersection_of(this_fields, next_fields, flags):
    fields_a = this_fields.astype(jnp.float32).reshape(this_fields.shape[0], KC, CW)
    fields_b = next_fields.astype(jnp.float32).reshape(next_fields.shape[0], KC, CW)
    summed = jnp.einsum('gkm,gkn->kmn', fields_a, fields_b, precision=lax.Precision.HIGHEST)
    return summed * tile_mask(flags, CW)

def reference(modes, exit_modes, pattern, attenuation, reflection):
    blocks = []
    for device in range(NS // SEC_DEV):
        merged = None
        for offset in range(SEC_DEV):
            section = device * SEC_DEV + offset
            next_fields = modes[section + 1] if section + 1 < NS else exit_modes
            unit_block = unit_matrices(intersection_of(modes[section], next_fields, pattern[section]), attenuation[section].reshape(KC, CW), reflection[section].reshape(KC, CW))
            merged = unit_block if merged is None else star_product(merged, unit_block)
        blocks.append(merged)
    while len(blocks) > 1:
        blocks = [star_product(blocks[2 * index], blocks[2 * index + 1]) for index in range(len(blocks) // 2)]
    return blocks[0]
```

```python
import functools

import jax
import jax.numpy as jnp
from jax import lax
from jax.experimental import pallas as pl
from jax.experimental.pallas import tpu as pltpu
from jax.sharding import PartitionSpec as P

BLOCK = 4
AXES = ("sec", "grid")


def halves(matrix):
    high = matrix.astype(jnp.bfloat16)
    return high, (matrix - high.astype(jnp.float32)).astype(jnp.bfloat16)


def mul(left, right, flip=False):
    dims = (((1,), (1 if flip else 0,)), ((), ()))

    def dot(a, b):
        return lax.dot_general(a, b, dims, preferred_element_type=jnp.float32)

    return dot(left[0], right[0]) + (dot(left[0], right[1]) + dot(left[1], right[0]))


def star_body(meta, *refs, orders, rows):
    terms, last, aux = refs[:BLOCK], refs[BLOCK], refs[BLOCK + 1 : 2 * BLOCK + 1]
    out, tbuf, abuf, rbuf = refs[2 * BLOCK + 1 :]
    for slot in range(BLOCK):
        tbuf[meta[slot]] = terms[slot][...]
        abuf[meta[BLOCK + slot]] = aux[slot][...]
    tbuf[BLOCK - 1] = last[...]
    width = out.shape[-1]
    picked = pl.ds(pl.multiple_of(meta[2 * BLOCK], 8), rows)
    row = lax.broadcasted_iota(jnp.int32, (width, width), 0)
    col = lax.broadcasted_iota(jnp.int32, (width, width), 1)
    part_row = lax.broadcasted_iota(jnp.int32, (rows, width), 0) + meta[2 * BLOCK]
    part_col = lax.broadcasted_iota(jnp.int32, (rows, width), 1)
    upper = jnp.logical_and(row < width // 2, col >= width // 2)
    lower = jnp.logical_and(row >= width // 2, col < width // 2)

    def diag(vector):
        return jnp.where(row == col, vector, 0.0)

    def part_diag(vector):
        return jnp.where(part_row == part_col, vector, 0.0)

    for order in range(orders):
        trans, front, back = [], [], []
        for sec in range(BLOCK):
            decay = abuf[sec, order, 0:1, :]
            mirror = abuf[sec, order, 1:2, :]
            mask = jnp.where(
                upper, abuf[sec, order, 2:3, :], jnp.where(lower, abuf[sec, order, 3:4, :], 1.0)
            )
            passing = jnp.broadcast_to(jnp.sqrt(1.0 - mirror * mirror), (width, width)).T
            trans.append(passing * (tbuf[sec, order] * mask) * decay)
            front.append(decay * decay * mirror)
            back.append(-mirror)
        bounce_a = back[0] * front[1]
        bounce_b = back[2] * front[3]
        gain_a = (1.0 + bounce_a * bounce_a) * (1.0 + bounce_a)
        gain_b = (1.0 + bounce_b * bounce_b) * (1.0 + bounce_b)
        flip_0 = trans[0].T
        flip_2 = trans[2].T
        rbuf[0] = flip_0
        rbuf[1] = trans[3]
        flip_0_part = rbuf[0, picked, :]
        trans_3_part = rbuf[1, picked, :]
        s0, s1, s2, s3 = [halves(t) for t in trans]
        trans_a = halves(mul(halves(trans[1] * gain_a), s0))
        back_a = halves(diag(back[1]) + mul(halves(trans[1] * (back[0] * gain_a)), s1, True))
        front_b = halves(diag(front[2]) + mul(halves(flip_2 * (front[3] * gain_b)), s2))
        trans_b = halves(mul(halves(trans[3] * gain_b), s2))
        flip_a_part = halves(mul(halves(flip_0_part * gain_a), s1, True))
        trans_b_part = mul(halves(trans_3_part * gain_b), s2)
        front_a_part = part_diag(front[0]) + mul(halves(flip_0_part * (front[1] * gain_a)), s0)
        back_b_part = part_diag(back[3]) + mul(halves(trans_3_part * (back[2] * gain_b)), s3, True)
        bounce = halves(mul(back_a, front_b))
        ahead = jnp.concatenate([trans_b_part, mul(flip_a_part, front_b)], axis=0)
        behind = mul(halves(trans_b_part), back_a)
        ahead = ahead + mul(halves(mul(halves(ahead), bounce)), bounce)
        behind = behind + mul(halves(mul(halves(behind), bounce, True)), bounce, True)
        ahead = ahead + mul(halves(ahead), bounce)
        behind = behind + mul(halves(behind), bounce, True)
        ahead = mul(halves(ahead), trans_a)
        out[0, order] = ahead[:rows]
        out[1, order] = front_a_part + ahead[rows:]
        out[2, order] = back_b_part + mul(halves(behind), trans_b, True)


def star_of_four(meta, terms, last, aux, rows):
    orders, width = last.shape[0], last.shape[-1]
    vmem = pl.BlockSpec(memory_space=pltpu.VMEM)
    return pl.pallas_call(
        functools.partial(star_body, orders=orders, rows=rows),
        out_shape=jax.ShapeDtypeStruct((3, orders, rows, width), jnp.float32),
        in_specs=[pl.BlockSpec(memory_space=pltpu.SMEM)] + [vmem] * (2 * BLOCK + 1),
        out_specs=vmem,
        scratch_shapes=[
            pltpu.VMEM((BLOCK + 1, orders, width, width), jnp.float32),
            pltpu.VMEM((BLOCK, orders) + aux[0].shape[1:], jnp.float32),
            pltpu.VMEM((2, width, width), jnp.float32),
        ],
        cost_estimate=pl.CostEstimate(
            flops=orders * 120 * width**3, bytes_accessed=orders * 8 * 4 * width**2, transcendentals=0
        ),
    )(meta, *terms, last, *aux)


def tall_dot(left, right):
    dims = (((0,), (0,)), ((), ()))
    return lax.dot_general(left, right, dims, preferred_element_type=jnp.float32)


def keep(outs, turn, item, value):
    for index, out in enumerate(outs):
        @pl.when(turn == index)
        def _():
            out[item] = value


def exit_body(place, own, after, *outs):
    keep(outs, pl.program_id(0), pl.program_id(1), tall_dot(own[...], after[...]))


def inner_body(place, own, before, after, *outs):
    turn, item = pl.program_id(0), pl.program_id(1)
    up = lax.rem(lax.rem(place[0] + turn, len(outs)), 2) == 0
    left = jnp.where(up, before[...], own[...])
    right = jnp.where(up, own[...], after[...])
    keep(outs, turn, item, tall_dot(left, right))


def partial_sums(body, place, operands, columns, count, orders, width):
    points = operands[0].shape[0]
    spot = lambda turn, place: lax.rem(place[0] + turn, count)
    specs = [
        pl.BlockSpec((points, width), lambda turn, item, place, col=col: (0, col(spot(turn, place), item)))
        for col in columns
    ]
    whole = pl.BlockSpec((orders, width, width), lambda turn, item, place: (0, 0, 0))
    return pl.pallas_call(
        body,
        out_shape=[jax.ShapeDtypeStruct((orders, width, width), jnp.float32)] * count,
        grid_spec=pltpu.PrefetchScalarGridSpec(
            num_scalar_prefetch=1, grid=(count, orders), in_specs=specs, out_specs=[whole] * count
        ),
        cost_estimate=pl.CostEstimate(
            flops=2 * count * orders * points * width**2,
            bytes_accessed=count * orders * width * (4 * points + 4 * width),
            transcendentals=0,
        ),
    )(place, *operands)


def body(modes, exit_modes, pattern, attenuation, reflection, *, chunks):
    sections, count = lax.axis_size("sec"), lax.axis_size("grid")
    sec, spot = lax.axis_index("sec"), lax.axis_index("grid")
    orders = pattern.shape[1]
    width = modes.shape[2] // orders
    share = orders // count
    fields = modes[0]
    place = jnp.reshape(spot, (1,)).astype(jnp.int32)
    everywhere = range(sections)

    def route(pairs):
        return [(s * count + g, t * count + h) for (s, g), (t, h) in pairs]

    def send(value, pairs):
        return lax.ppermute(value, AXES, route(pairs))

    def summed(parts, secs):
        total = parts[0]
        for turn in range(1, count):
            pairs = [((s, g), (s, (g + turn) % count)) for s in secs for g in range(count)]
            total = total + send(parts[turn], pairs)
        return total

    def columns(parity, items):
        return jnp.concatenate(
            [
                fields[:, (g * share + j) * width : (g * share + j + 1) * width]
                for g in range(parity, count, 2)
                for j in items
            ],
            axis=1,
        )

    arrived = []
    for items in chunks:
        ups = [((s, g), (s + 1, g)) for s in range(sections - 1) for g in range(count)]
        downs = [((s + 1, g), (s, g)) for s in range(sections - 1) for g in range(count)]
        arrived.append((send(columns(0, items), ups), send(columns(1, items), downs)))

    def own_orders(value):
        return lax.dynamic_slice_in_dim(value, spot * share, share, 0)

    rows_of = [own_orders(attenuation.reshape(orders, width)), own_orders(reflection.reshape(orders, width))]
    flags = own_orders(pattern[0]).astype(jnp.float32)
    rows_of += [jnp.broadcast_to(flags[:, side : side + 1], (share, width)) for side in (0, 1)]
    aux = jnp.stack(rows_of, axis=1)
    ring = [
        [(s, s - s % BLOCK + (s + turn) % BLOCK) for s in everywhere] for turn in range(BLOCK)
    ]
    all_aux = [aux] + [
        send(aux, [((s, g), (t, g)) for s, t in ring[turn] for g in range(count)]) for turn in range(1, BLOCK)
    ]

    final = sections - 1
    exit_columns = [lambda at, item: at * share + item] * 2
    exit_parts = partial_sums(exit_body, place, (fields, exit_modes), exit_columns, count, share, width)
    last = summed(exit_parts, [final])
    at_end = sec == final
    if sections == BLOCK:
        got = send(last, [((final, g), (final - 2, g)) for g in range(count)])
        held = jnp.where(at_end, last, got)
        hops = [(final, final - 1), (final - 2, final - 3)]
        got = send(held, [((s, g), (t, g)) for s, t in hops for g in range(count)])
        last = jnp.where(jnp.logical_or(at_end, sec == final - 2), held, got)

    odd = spot % 2
    results = []
    for items, (before, after) in zip(chunks, arrived):
        number = len(items)
        columns_of = [
            lambda at, item, first=items[0]: at * share + first + item,
            lambda at, item, number=number: lax.div(at, 2) * number + item,
            lambda at, item, number=number: lax.div(at, 2) * number + item,
        ]
        parts = partial_sums(inner_body, place, (fields, before, after), columns_of, count, number, width)
        own = summed(parts, everywhere)
        tail = last[items[0] : items[0] + number]
        some_aux = [a[items[0] : items[0] + number] for a in all_aux]
        if sections == BLOCK:
            holds = lambda s, g: s > 0 if g % 2 == 0 else s < final
            terms = [own] + [
                send(own, [((s, g), (t, g)) for s, t in ring[turn] for g in range(count) if holds(s, g)])
                for turn in range(1, BLOCK)
            ]
            shifted = 1 - odd
            rows = width // sections
            first_row = sec * rows
        else:
            back = send(own, [((s + 1, g), (s, g)) for s in range(final) for g in range(0, count, 2)])
            own = jnp.where(at_end, tail, jnp.where(odd == 0, back, own))
            terms = [own] + [
                send(own, [((s, g), (t, g)) for s, t in ring[turn] for g in range(count)])
                for turn in range(1, BLOCK)
            ]
            shifted = 0
            rows, first_row = width, 0
        froms = [(sec - turn) % BLOCK for turn in range(BLOCK)]
        if sections != BLOCK:
            tail = sum(jnp.where(f == BLOCK - 1, t, 0.0) for f, t in zip(froms, terms))
        meta = jnp.stack([(f - shifted) % (BLOCK + 1) for f in froms] + froms + [first_row + 0 * sec])
        merged = star_of_four(meta.astype(jnp.int32), terms, tail, some_aux, rows)
        results.append(merged)
    merged = jnp.concatenate(results, axis=1) if len(results) > 1 else results[0]
    if sections > BLOCK:
        merged = later_levels(merged, sections, sec)
    return merged


def pair_body(first, second, out):
    for order in range(out.shape[1]):
        trans_a, front_a, back_a = (first[i, order] for i in range(3))
        trans_b, front_b, back_b = (second[i, order] for i in range(3))
        bounce = halves(mul(halves(back_a), halves(front_b)))
        square = halves(mul(bounce, bounce))
        inner = trans_a + mul(bounce, halves(trans_a))
        inner = halves(inner + mul(square, halves(inner)))
        behind = trans_b + mul(halves(trans_b), bounce)
        behind = halves(behind + mul(halves(behind), square))
        left = halves(trans_b)
        out[0, order] = mul(left, inner)
        out[1, order] = front_a + mul(halves(trans_a.T), halves(mul(halves(front_b), inner)))
        out[2, order] = back_b + mul(left, halves(mul(halves(back_a), behind, True)))


def later_levels(merged, sections, sec):
    vmem = pl.BlockSpec(memory_space=pltpu.VMEM)
    star = pl.pallas_call(
        pair_body, out_shape=jax.ShapeDtypeStruct(merged.shape, merged.dtype), in_specs=[vmem] * 2, out_specs=vmem
    )
    stride = BLOCK
    while stride < sections:
        other = lax.ppermute(merged, "sec", [(s, s ^ stride) for s in range(sections)])
        high = lax.rem(lax.div(sec, stride), 2) == 1
        merged = star(jnp.where(high, other, merged), jnp.where(high, merged, other))
        stride *= 2
    rows = merged.shape[2] // sections
    return lax.dynamic_slice_in_dim(merged, sec * rows, rows, 2)


def solution(mesh):
    share = 8 // mesh.shape["grid"]
    chunks = [list(range(share))]
    in_specs = (
        P(("groups", "sec"), "grid", None),
        P(("groups", "grid"), None),
        P(("groups", "sec"), None, None),
        P(("groups", "sec"), None),
        P(("groups", "sec"), None),
    )
    out_specs = P("groups", "grid", "sec", None)
    step = functools.partial(body, chunks=chunks)
    return jax.shard_map(step, mesh=mesh, in_specs=in_specs, out_specs=out_specs, check_vma=False)
```

```python
import functools

import jax
import jax.numpy as jnp
from jax import lax
from jax.experimental import pallas as pl
from jax.experimental.pallas import tpu as pltpu
from jax.sharding import PartitionSpec as P

CHUNKS = lambda share: [list(range(share))]
BLOCK = 4
AXES = ("sec", "grid")
ROOM = pltpu.CompilerParams(vmem_limit_bytes=16 * 2**20)


def halves(matrix):
    high = matrix.astype(jnp.bfloat16)
    return high, (matrix - high.astype(jnp.float32)).astype(jnp.bfloat16)


def mul(left, right, flip=False):
    dims = (((1,), (1 if flip else 0,)), ((), ()))

    def dot(a, b):
        return lax.dot_general(a, b, dims, preferred_element_type=jnp.float32)

    return dot(left[0], right[0]) + (dot(left[0], right[1]) + dot(left[1], right[0]))


def star_body(meta, *refs, orders, rows, earlier):
    terms, last, aux = refs[:BLOCK], refs[BLOCK], refs[BLOCK + 1 : 2 * BLOCK + 1]
    done = refs[2 * BLOCK + 1 : -4]
    out, tbuf, abuf, rbuf = refs[-4:]
    for ready in done:
        out[:, :earlier] = ready[...]
    for slot in range(BLOCK):
        tbuf[meta[slot]] = terms[slot][...]
        abuf[meta[BLOCK + slot]] = aux[slot][...]
    tbuf[BLOCK - 1] = last[...]
    width = out.shape[-1]
    picked = pl.ds(pl.multiple_of(meta[2 * BLOCK], 8), rows)
    row = lax.broadcasted_iota(jnp.int32, (width, width), 0)
    col = lax.broadcasted_iota(jnp.int32, (width, width), 1)
    part_row = lax.broadcasted_iota(jnp.int32, (rows, width), 0) + meta[2 * BLOCK]
    part_col = lax.broadcasted_iota(jnp.int32, (rows, width), 1)
    upper = jnp.logical_and(row < width // 2, col >= width // 2)
    lower = jnp.logical_and(row >= width // 2, col < width // 2)

    def diag(vector):
        return jnp.where(row == col, vector, 0.0)

    def part_diag(vector):
        return jnp.where(part_row == part_col, vector, 0.0)

    for order in range(orders):
        trans, front, back = [], [], []
        for sec in range(BLOCK):
            decay = abuf[sec, order, 0:1, :]
            mirror = abuf[sec, order, 1:2, :]
            mask = jnp.where(
                upper, abuf[sec, order, 2:3, :], jnp.where(lower, abuf[sec, order, 3:4, :], 1.0)
            )
            passing = jnp.broadcast_to(jnp.sqrt(1.0 - mirror * mirror), (width, width)).T
            trans.append(passing * (tbuf[sec, order] * mask) * decay)
            front.append(decay * decay * mirror)
            back.append(-mirror)
        bounce_a = back[0] * front[1]
        bounce_b = back[2] * front[3]
        gain_a = (1.0 + bounce_a * bounce_a) * (1.0 + bounce_a)
        gain_b = (1.0 + bounce_b * bounce_b) * (1.0 + bounce_b)
        flip_0 = trans[0].T
        flip_2 = trans[2].T
        rbuf[0] = flip_0
        rbuf[1] = trans[3]
        flip_0_part = rbuf[0, picked, :]
        trans_3_part = rbuf[1, picked, :]
        s0, s1, s2, s3 = [halves(t) for t in trans]
        trans_a = halves(mul(halves(trans[1] * gain_a), s0))
        back_a = halves(diag(back[1]) + mul(halves(trans[1] * (back[0] * gain_a)), s1, True))
        front_b = halves(diag(front[2]) + mul(halves(flip_2 * (front[3] * gain_b)), s2))
        trans_b = halves(mul(halves(trans[3] * gain_b), s2))
        flip_a_part = halves(mul(halves(flip_0_part * gain_a), s1, True))
        trans_b_part = mul(halves(trans_3_part * gain_b), s2)
        front_a_part = part_diag(front[0]) + mul(halves(flip_0_part * (front[1] * gain_a)), s0)
        back_b_part = part_diag(back[3]) + mul(halves(trans_3_part * (back[2] * gain_b)), s3, True)
        bounce = halves(mul(back_a, front_b))
        ahead = jnp.concatenate([trans_b_part, mul(flip_a_part, front_b)], axis=0)
        behind = mul(halves(trans_b_part), back_a)
        ahead = ahead + mul(halves(mul(halves(ahead), bounce)), bounce)
        behind = behind + mul(halves(mul(halves(behind), bounce, True)), bounce, True)
        ahead = ahead + mul(halves(ahead), bounce)
        behind = behind + mul(halves(behind), bounce, True)
        ahead = mul(halves(ahead), trans_a)
        out[0, earlier + order] = ahead[:rows]
        out[1, earlier + order] = front_a_part + ahead[rows:]
        out[2, earlier + order] = back_b_part + mul(halves(behind), trans_b, True)


def star_of_four(meta, terms, last, aux, rows, done):
    orders, width = last.shape[0], last.shape[-1]
    earlier = sum(ready.shape[1] for ready in done)
    vmem = pl.BlockSpec(memory_space=pltpu.VMEM)
    return pl.pallas_call(
        functools.partial(star_body, orders=orders, rows=rows, earlier=earlier),
        out_shape=jax.ShapeDtypeStruct((3, earlier + orders, rows, width), jnp.float32),
        in_specs=[pl.BlockSpec(memory_space=pltpu.SMEM)] + [vmem] * (2 * BLOCK + 1 + len(done)),
        out_specs=vmem,
        scratch_shapes=[
            pltpu.VMEM((BLOCK + 1, orders, width, width), jnp.float32),
            pltpu.VMEM((BLOCK, orders) + aux[0].shape[1:], jnp.float32),
            pltpu.VMEM((2, width, width), jnp.float32),
        ],
        compiler_params=ROOM,
        cost_estimate=pl.CostEstimate(
            flops=orders * 120 * width**3, bytes_accessed=orders * 8 * 4 * width**2, transcendentals=0
        ),
    )(meta, *terms, last, *aux, *done)


def tall_dot(left, right):
    dims = (((0,), (0,)), ((), ()))
    return lax.dot_general(left, right, dims, preferred_element_type=jnp.float32)


def hand_out(place, terms, outs):
    count = len(outs)
    for turn, out in enumerate(outs):
        out[...] = terms[lax.rem(place[0] + turn, count)]


def exit_body(place, own, after, *refs):
    outs, terms = refs[:-1], refs[-1]
    count, share, width = terms.shape[:3]
    for spot in range(count):
        for item in range(share):
            columns = pl.ds((spot * share + item) * width, width)
            terms[spot, item] = tall_dot(own[:, columns], after[:, columns])
    hand_out(place, terms, outs)


def exit_sums(place, fields, exit_modes, count, share, width):
    points, modes = fields.shape
    whole = pl.BlockSpec(memory_space=pltpu.VMEM)
    return pl.pallas_call(
        exit_body,
        out_shape=[jax.ShapeDtypeStruct((share, width, width), jnp.float32)] * count,
        in_specs=[pl.BlockSpec(memory_space=pltpu.SMEM), whole, whole],
        out_specs=[whole] * count,
        scratch_shapes=[pltpu.VMEM((count, share, width, width), jnp.float32)],
        compiler_params=ROOM,
        cost_estimate=pl.CostEstimate(
            flops=2 * points * modes * width, bytes_accessed=4 * points * modes, transcendentals=0
        ),
    )(place, fields, exit_modes)


def inner_body(place, fields, before, after, *refs, items, share):
    outs, terms = refs[:-1], refs[-1]
    count, number, width = terms.shape[:3]
    for spot in range(count):
        for index, item in enumerate(items):
            own = fields[:, pl.ds((spot * share + item) * width, width)]
            columns = pl.ds((spot // 2 * number + index) * width, width)
            if spot % 2 == 0:
                terms[spot, index] = tall_dot(before[:, columns], own)
            else:
                terms[spot, index] = tall_dot(own, after[:, columns])
    hand_out(place, terms, outs)


def inner_sums(place, fields, before, after, count, share, items, width):
    points, number = fields.shape[0], len(items)
    whole = pl.BlockSpec(memory_space=pltpu.VMEM)
    return pl.pallas_call(
        functools.partial(inner_body, items=items, share=share),
        out_shape=[jax.ShapeDtypeStruct((number, width, width), jnp.float32)] * count,
        in_specs=[pl.BlockSpec(memory_space=pltpu.SMEM), whole, whole, whole],
        out_specs=[whole] * count,
        scratch_shapes=[pltpu.VMEM((count, number, width, width), jnp.float32)],
        compiler_params=ROOM,
        cost_estimate=pl.CostEstimate(
            flops=2 * count * number * points * width**2,
            bytes_accessed=count * number * width * (4 * points + 4 * width),
            transcendentals=0,
        ),
    )(place, fields, before, after)


def pack_body(fields, *refs, items, share, width):
    outs, semaphores = refs[:-1], refs[-1]
    number = len(items)
    copies = []
    for spot in range(semaphores.shape[0]):
        source = pl.ds((spot * share + items[0]) * width, number * width)
        target = pl.ds(spot // 2 * number * width, number * width)
        copy = pltpu.make_async_copy(
            fields.at[:, source], outs[spot % 2].at[:, target], semaphores.at[spot]
        )
        copy.start()
        copies.append(copy)
    for copy in copies:
        copy.wait()


def packed(fields, count, share, items, width):
    far = pl.BlockSpec(memory_space=pl.ANY)
    shape = (fields.shape[0], count // 2 * len(items) * width)
    return pl.pallas_call(
        functools.partial(pack_body, items=items, share=share, width=width),
        out_shape=[jax.ShapeDtypeStruct(shape, fields.dtype)] * 2,
        in_specs=[far],
        out_specs=[far] * 2,
        scratch_shapes=[pltpu.SemaphoreType.DMA((count,))],
        compiler_params=ROOM,
        cost_estimate=pl.CostEstimate(flops=0, bytes_accessed=8 * shape[0] * shape[1], transcendentals=0),
    )(fields)


def body(modes, exit_modes, pattern, attenuation, reflection, *, chunks):
    sections, count = lax.axis_size("sec"), lax.axis_size("grid")
    sec, spot = lax.axis_index("sec"), lax.axis_index("grid")
    orders = pattern.shape[1]
    width = modes.shape[2] // orders
    share = orders // count
    fields = modes[0]
    place = jnp.reshape(spot, (1,)).astype(jnp.int32)
    everywhere = range(sections)

    def route(pairs):
        return [(s * count + g, t * count + h) for (s, g), (t, h) in pairs]

    def send(value, pairs):
        return lax.ppermute(value, AXES, route(pairs))

    def summed(parts, secs):
        total = parts[0]
        for turn in range(1, count):
            pairs = [((s, g), (s, (g + turn) % count)) for s in secs for g in range(count)]
            total = total + send(parts[turn], pairs)
        return total

    ups = [((s, g), (s + 1, g)) for s in range(sections - 1) for g in range(count)]
    downs = [(t, s) for s, t in ups]
    arrived, source = [], fields
    for items in chunks:
        for_up, for_down = packed(source, count, share, items, width)
        source, for_up, for_down = lax.optimization_barrier((fields, for_up, for_down))
        arrived.append((send(for_up, ups), send(for_down, downs)))

    def own_orders(value):
        return lax.dynamic_slice_in_dim(value, spot * share, share, 0)

    rows_of = [own_orders(attenuation.reshape(orders, width)), own_orders(reflection.reshape(orders, width))]
    flags = own_orders(pattern[0]).astype(jnp.float32)
    rows_of += [jnp.broadcast_to(flags[:, side : side + 1], (share, width)) for side in (0, 1)]
    aux = jnp.stack(rows_of, axis=1)
    ring = [
        [(s, s - s % BLOCK + (s + turn) % BLOCK) for s in everywhere] for turn in range(BLOCK)
    ]
    all_aux = [aux] + [
        send(aux, [((s, g), (t, g)) for s, t in ring[turn] for g in range(count)]) for turn in range(1, BLOCK)
    ]

    final = sections - 1
    exit_parts = exit_sums(place, fields, exit_modes, count, share, width)
    last = summed(exit_parts, [final])
    at_end = sec == final
    if sections == BLOCK:
        got = send(last, [((final, g), (final - 2, g)) for g in range(count)])
        held = jnp.where(at_end, last, got)
        hops = [(final, final - 1), (final - 2, final - 3)]
        got = send(held, [((s, g), (t, g)) for s, t in hops for g in range(count)])
        last = jnp.where(jnp.logical_or(at_end, sec == final - 2), held, got)

    odd = spot % 2
    done = []
    for items, (before, after) in zip(chunks, arrived):
        number = len(items)
        parts = inner_sums(place, fields, before, after, count, share, items, width)
        own = summed(parts, everywhere)
        if items is not chunks[-1]:
            own = lax.optimization_barrier((own,) + arrived[-1])[0]
        tail = last[items[0] : items[0] + number]
        some_aux = [a[items[0] : items[0] + number] for a in all_aux]
        if sections == BLOCK:
            holds = lambda s, g: s > 0 if g % 2 == 0 else s < final
            terms = [own] + [
                send(own, [((s, g), (t, g)) for s, t in ring[turn] for g in range(count) if holds(s, g)])
                for turn in range(1, BLOCK)
            ]
            shifted = 1 - odd
            rows = width // sections
            first_row = sec * rows
        else:
            back = send(own, [((s + 1, g), (s, g)) for s in range(final) for g in range(0, count, 2)])
            own = jnp.where(at_end, tail, jnp.where(odd == 0, back, own))
            terms = [own] + [
                send(own, [((s, g), (t, g)) for s, t in ring[turn] for g in range(count)])
                for turn in range(1, BLOCK)
            ]
            shifted = 0
            rows, first_row = width, 0
        froms = [(sec - turn) % BLOCK for turn in range(BLOCK)]
        if sections != BLOCK:
            tail = sum(jnp.where(f == BLOCK - 1, t, 0.0) for f, t in zip(froms, terms))
        meta = jnp.stack([(f - shifted) % (BLOCK + 1) for f in froms] + froms + [first_row + 0 * sec])
        merged = star_of_four(meta.astype(jnp.int32), terms, tail, some_aux, rows, done)
        done = [merged]
    if sections > BLOCK:
        merged = later_levels(merged, sections, sec)
    return merged


def pair_body(first, second, out):
    for order in range(out.shape[1]):
        trans_a, front_a, back_a = (first[i, order] for i in range(3))
        trans_b, front_b, back_b = (second[i, order] for i in range(3))
        bounce = halves(mul(halves(back_a), halves(front_b)))
        square = halves(mul(bounce, bounce))
        inner = trans_a + mul(bounce, halves(trans_a))
        inner = halves(inner + mul(square, halves(inner)))
        behind = trans_b + mul(halves(trans_b), bounce)
        behind = halves(behind + mul(halves(behind), square))
        left = halves(trans_b)
        out[0, order] = mul(left, inner)
        out[1, order] = front_a + mul(halves(trans_a.T), halves(mul(halves(front_b), inner)))
        out[2, order] = back_b + mul(left, halves(mul(halves(back_a), behind, True)))


def later_levels(merged, sections, sec):
    vmem = pl.BlockSpec(memory_space=pltpu.VMEM)
    star = pl.pallas_call(
        pair_body, out_shape=jax.ShapeDtypeStruct(merged.shape, merged.dtype), in_specs=[vmem] * 2, out_specs=vmem
    )
    stride = BLOCK
    while stride < sections:
        other = lax.ppermute(merged, "sec", [(s, s ^ stride) for s in range(sections)])
        high = lax.rem(lax.div(sec, stride), 2) == 1
        merged = star(jnp.where(high, other, merged), jnp.where(high, merged, other))
        stride *= 2
    rows = merged.shape[2] // sections
    return lax.dynamic_slice_in_dim(merged, sec * rows, rows, 2)


def solution(mesh):
    share = 8 // mesh.shape["grid"]
    chunks = CHUNKS(share)
    in_specs = (
        P(("groups", "sec"), "grid", None),
        P(("groups", "grid"), None),
        P(("groups", "sec"), None, None),
        P(("groups", "sec"), None),
        P(("groups", "sec"), None),
    )
    out_specs = P("groups", "grid", "sec", None)
    step = functools.partial(body, chunks=chunks)
    return jax.shard_map(step, mesh=mesh, in_specs=in_specs, out_specs=out_specs, check_vma=False)
```

```python
import functools

import jax
import jax.numpy as jnp
from jax import lax
from jax.experimental import pallas as pl
from jax.experimental.pallas import tpu as pltpu
from jax.sharding import PartitionSpec as P

BLOCK = 4
AXES = ("sec", "grid")
ROOM = pltpu.CompilerParams(vmem_limit_bytes=16 * 2**20)


def halves(matrix):
    high = matrix.astype(jnp.bfloat16)
    return high, (matrix - high.astype(jnp.float32)).astype(jnp.bfloat16)


def mul(left, right, flip=False):
    dims = (((1,), (1 if flip else 0,)), ((), ()))

    def dot(a, b):
        return lax.dot_general(a, b, dims, preferred_element_type=jnp.float32)

    return dot(left[0], right[0]) + (dot(left[0], right[1]) + dot(left[1], right[0]))


def star_body(place, *refs, orders, rows):
    terms = refs[:BLOCK]
    out, tbuf, abuf, rbuf = refs[BLOCK:]
    width = out.shape[-1]
    for slot in range(BLOCK):
        origin = lax.rem(place[1] + BLOCK - slot, BLOCK)
        tbuf[lax.rem(origin + BLOCK - place[2], BLOCK)] = terms[slot][:, :width]
        abuf[origin] = terms[slot][:, width:]
    first_row = place[1] * rows if rows < width else 0
    picked = pl.ds(pl.multiple_of(first_row, 8), rows) if rows < width else pl.ds(0, rows)
    row = lax.broadcasted_iota(jnp.int32, (width, width), 0)
    col = lax.broadcasted_iota(jnp.int32, (width, width), 1)
    part_row = lax.broadcasted_iota(jnp.int32, (rows, width), 0) + first_row
    part_col = lax.broadcasted_iota(jnp.int32, (rows, width), 1)
    upper = jnp.logical_and(row < width // 2, col >= width // 2)
    lower = jnp.logical_and(row >= width // 2, col < width // 2)

    def diag(vector):
        return jnp.where(row == col, vector, 0.0)

    def part_diag(vector):
        return jnp.where(part_row == part_col, vector, 0.0)

    for order in range(orders):
        trans, front, back = [], [], []
        for sec in range(BLOCK):
            decay = abuf[sec, order, 0:1, :]
            mirror = abuf[sec, order, 1:2, :]
            mask = jnp.where(
                upper, abuf[sec, order, 2:3, :], jnp.where(lower, abuf[sec, order, 3:4, :], 1.0)
            )
            passing = jnp.broadcast_to(jnp.sqrt(1.0 - mirror * mirror), (width, width)).T
            trans.append(passing * (tbuf[sec, order] * mask) * decay)
            front.append(decay * decay * mirror)
            back.append(-mirror)
        bounce_a = back[0] * front[1]
        bounce_b = back[2] * front[3]
        gain_a = (1.0 + bounce_a * bounce_a) * (1.0 + bounce_a)
        gain_b = (1.0 + bounce_b * bounce_b) * (1.0 + bounce_b)
        flip_0 = trans[0].T
        flip_2 = trans[2].T
        rbuf[0] = flip_0
        rbuf[1] = trans[3]
        flip_0_part = rbuf[0, picked, :]
        trans_3_part = rbuf[1, picked, :]
        s0, s1, s2, s3 = [halves(t) for t in trans]
        trans_a = halves(mul(halves(trans[1] * gain_a), s0))
        back_a = halves(diag(back[1]) + mul(halves(trans[1] * (back[0] * gain_a)), s1, True))
        front_b = halves(diag(front[2]) + mul(halves(flip_2 * (front[3] * gain_b)), s2))
        trans_b = halves(mul(halves(trans[3] * gain_b), s2))
        flip_a_part = halves(mul(halves(flip_0_part * gain_a), s1, True))
        trans_b_part = mul(halves(trans_3_part * gain_b), s2)
        front_a_part = part_diag(front[0]) + mul(halves(flip_0_part * (front[1] * gain_a)), s0)
        back_b_part = part_diag(back[3]) + mul(halves(trans_3_part * (back[2] * gain_b)), s3, True)
        bounce = halves(mul(back_a, front_b))
        ahead = jnp.concatenate([trans_b_part, mul(flip_a_part, front_b)], axis=0)
        behind = mul(halves(trans_b_part), back_a)
        ahead = ahead + mul(halves(mul(halves(ahead), bounce)), bounce)
        behind = behind + mul(halves(mul(halves(behind), bounce, True)), bounce, True)
        ahead = ahead + mul(halves(ahead), bounce)
        behind = behind + mul(halves(behind), bounce, True)
        ahead = mul(halves(ahead), trans_a)
        out[0, order] = ahead[:rows]
        out[1, order] = front_a_part + ahead[rows:]
        out[2, order] = back_b_part + mul(halves(behind), trans_b, True)


def star_of_four(place, terms, rows):
    orders, width = terms[0].shape[0], terms[0].shape[-1]
    extra = terms[0].shape[1] - width
    vmem = pl.BlockSpec(memory_space=pltpu.VMEM)
    return pl.pallas_call(
        functools.partial(star_body, orders=orders, rows=rows),
        out_shape=jax.ShapeDtypeStruct((3, orders, rows, width), jnp.float32),
        in_specs=[pl.BlockSpec(memory_space=pltpu.SMEM)] + [vmem] * BLOCK,
        out_specs=vmem,
        scratch_shapes=[
            pltpu.VMEM((BLOCK, orders, width, width), jnp.float32),
            pltpu.VMEM((BLOCK, orders, extra, width), jnp.float32),
            pltpu.VMEM((2, width, width), jnp.float32),
        ],
        compiler_params=ROOM,
        cost_estimate=pl.CostEstimate(
            flops=orders * 120 * width**3, bytes_accessed=orders * 8 * 4 * width**2, transcendentals=0
        ),
    )(place, *terms)


def own_body(place, pattern, decays, mirrors, *refs):
    parts, (exits, hop, out) = refs[:-3], refs[-3:]
    width = out.shape[-1]
    out[:, width:] = jnp.zeros_like(out[:, width:])
    share = out.shape[0]
    for index in range(share):
        total = parts[0][index]
        for part in parts[1:]:
            total = total + part[index]
        total = jnp.where(place[3] == 1, exits[index], total)
        out[index, :width] = jnp.where(place[3] == 2, hop[index], total)
        order = place[0] * share + index
        columns = pl.ds(pl.multiple_of(order * width, width), width)
        out[index, width : width + 1] = decays[:, columns]
        out[index, width + 1 : width + 2] = mirrors[:, columns]
        for side in (0, 1):
            flag = pattern[0, order, side].astype(jnp.float32)
            out[index, width + 2 + side : width + 3 + side] = jnp.full((1, width), flag)


def own_terms(place, pattern, decays, mirrors, parts, exits, hop):
    number, width = parts[0].shape[0], parts[0].shape[-1]
    vmem, smem = pl.BlockSpec(memory_space=pltpu.VMEM), pl.BlockSpec(memory_space=pltpu.SMEM)
    return pl.pallas_call(
        own_body,
        out_shape=jax.ShapeDtypeStruct((number, width + 8, width), jnp.float32),
        in_specs=[smem] * 2 + [vmem] * (4 + len(parts)),
        out_specs=vmem,
        compiler_params=ROOM,
        cost_estimate=pl.CostEstimate(
            flops=4 * number * width**2, bytes_accessed=28 * number * width**2, transcendentals=0
        ),
    )(place, pattern, decays, mirrors, *parts, exits, hop)


def tall_dot(left, right):
    dims = (((0,), (0,)), ((), ()))
    return lax.dot_general(left, right, dims, preferred_element_type=jnp.float32)


def hand_out(place, terms, outs):
    count = len(outs)
    for turn, out in enumerate(outs):
        out[...] = terms[lax.rem(place[0] + turn, count)]


def exit_body(place, own, after, *refs):
    outs, terms = refs[:-1], refs[-1]
    count, share, width = terms.shape[:3]
    for spot in range(count):
        for item in range(share):
            columns = pl.ds((spot * share + item) * width, width)
            terms[spot, item] = tall_dot(own[:, columns], after[:, columns])
    hand_out(place, terms, outs)


def exit_sums(place, fields, exit_modes, count, share, width):
    points, modes = fields.shape
    whole = pl.BlockSpec(memory_space=pltpu.VMEM)
    return pl.pallas_call(
        exit_body,
        out_shape=[jax.ShapeDtypeStruct((share, width, width), jnp.float32)] * count,
        in_specs=[pl.BlockSpec(memory_space=pltpu.SMEM), whole, whole],
        out_specs=[whole] * count,
        scratch_shapes=[pltpu.VMEM((count, share, width, width), jnp.float32)],
        compiler_params=ROOM,
        cost_estimate=pl.CostEstimate(
            flops=2 * points * modes * width, bytes_accessed=4 * points * modes, transcendentals=0
        ),
    )(place, fields, exit_modes)


def inner_body(place, fields, arrived, *refs):
    outs, terms = refs[:-1], refs[-1]
    count, share, width = terms.shape[:3]

    def fill(left, right):
        for order in range(count * share):
            columns = pl.ds(order * width, width)
            terms[order // share, order % share] = tall_dot(left[:, columns], right[:, columns])

    even = lax.rem(place[0], 2) == 0

    @pl.when(even)
    def _():
        fill(arrived, fields)

    @pl.when(jnp.logical_not(even))
    def _():
        fill(fields, arrived)

    hand_out(place, terms, outs)


def inner_sums(place, fields, arrived, count, share, width):
    points, modes = fields.shape
    whole = pl.BlockSpec(memory_space=pltpu.VMEM)
    return pl.pallas_call(
        inner_body,
        out_shape=[jax.ShapeDtypeStruct((share, width, width), jnp.float32)] * count,
        in_specs=[pl.BlockSpec(memory_space=pltpu.SMEM), whole, whole],
        out_specs=[whole] * count,
        scratch_shapes=[pltpu.VMEM((count, share, width, width), jnp.float32)],
        compiler_params=ROOM,
        cost_estimate=pl.CostEstimate(
            flops=2 * points * modes * width, bytes_accessed=4 * points * modes, transcendentals=0
        ),
    )(place, fields, arrived)


def body(modes, exit_modes, pattern, attenuation, reflection):
    sections, count = lax.axis_size("sec"), lax.axis_size("grid")
    sec, spot = lax.axis_index("sec"), lax.axis_index("grid")
    orders = pattern.shape[1]
    width = modes.shape[2] // orders
    share = orders // count
    fields = modes[0]
    final = sections - 1
    small = sections == BLOCK
    even = 1 - lax.rem(spot, 2)
    if small:
        late = even
        special = jnp.where(even == 1, jnp.where(sec == 0, 2, 0), jnp.where(sec == final, 1, 0))
    else:
        late = 0 * even
        special = jnp.where(sec == final, 1, 0)
    place = jnp.stack([spot, sec, late, special]).astype(jnp.int32)

    def send(value, pairs):
        return lax.ppermute(value, AXES, [(s * count + g, t * count + h) for (s, g), (t, h) in pairs])

    def gathered(parts, members):
        got = [parts[0]]
        for turn in range(1, count):
            got.append(send(parts[turn], [(row[g], row[(g + turn) % count]) for row in members for g in range(count)]))
        return got

    steps = [((s + g % 2, g), (s + 1 - g % 2, g)) for s in range(final) for g in range(count)]
    arrived = send(fields, steps)

    exit_parts = exit_sums(place, fields, exit_modes, count, share, width)
    exits = sum(gathered(exit_parts, [[(final, g) for g in range(count)]]))
    hop = send(exits, [((final, g), (0, g)) for g in range(0, count, 2)]) if small else exits

    parts = inner_sums(place, fields, arrived, count, share, width)
    parts = gathered(parts, [[(s + 1 - g % 2, g) for g in range(count)] for s in range(final)])
    if not small:
        own = sum(parts)
        back = send(own, [((s + 1, g), (s, g)) for s in range(final) for g in range(0, count, 2)])
        parts = [jnp.where(even == 1, back, own)]
    own = own_terms(place, pattern, attenuation, reflection, parts, exits, hop)
    terms = [own]
    for turn in range(1, BLOCK):
        ring = [(s, s - s % BLOCK + (s + turn) % BLOCK) for s in range(sections)]
        terms.append(send(own, [((s, g), (t, g)) for s, t in ring for g in range(count)]))
    merged = star_of_four(place, terms, width // sections if small else width)
    return merged if small else later_levels(merged, sections, sec)


def pair_body(first, second, out):
    for order in range(out.shape[1]):
        trans_a, front_a, back_a = (first[i, order] for i in range(3))
        trans_b, front_b, back_b = (second[i, order] for i in range(3))
        bounce = halves(mul(halves(back_a), halves(front_b)))
        square = halves(mul(bounce, bounce))
        inner = trans_a + mul(bounce, halves(trans_a))
        inner = halves(inner + mul(square, halves(inner)))
        behind = trans_b + mul(halves(trans_b), bounce)
        behind = halves(behind + mul(halves(behind), square))
        left = halves(trans_b)
        out[0, order] = mul(left, inner)
        out[1, order] = front_a + mul(halves(trans_a.T), halves(mul(halves(front_b), inner)))
        out[2, order] = back_b + mul(left, halves(mul(halves(back_a), behind, True)))


def later_levels(merged, sections, sec):
    vmem = pl.BlockSpec(memory_space=pltpu.VMEM)
    star = pl.pallas_call(
        pair_body, out_shape=jax.ShapeDtypeStruct(merged.shape, merged.dtype), in_specs=[vmem] * 2, out_specs=vmem
    )
    stride = BLOCK
    while stride < sections:
        other = lax.ppermute(merged, "sec", [(s, s ^ stride) for s in range(sections)])
        high = lax.rem(lax.div(sec, stride), 2) == 1
        merged = star(jnp.where(high, other, merged), jnp.where(high, merged, other))
        stride *= 2
    rows = merged.shape[2] // sections
    return lax.dynamic_slice_in_dim(merged, sec * rows, rows, 2)


def solution(mesh):
    in_specs = (
        P(("groups", "sec"), "grid", None),
        P(("groups", "grid"), None),
        P(("groups", "sec"), None, None),
        P(("groups", "sec"), None),
        P(("groups", "sec"), None),
    )
    out_specs = P("groups", "grid", "sec", None)
    return jax.shard_map(body, mesh=mesh, in_specs=in_specs, out_specs=out_specs, check_vma=False)
```

```python
import functools

import jax
import jax.numpy as jnp
from jax import lax
from jax.experimental import pallas as pl
from jax.experimental.pallas import tpu as pltpu
from jax.sharding import PartitionSpec as P

BLOCK = 4
AXES = ("sec", "grid")
ROOM = pltpu.CompilerParams(vmem_limit_bytes=16 * 2**20)


def halves(matrix):
    high = matrix.astype(jnp.bfloat16)
    return high, (matrix - high.astype(jnp.float32)).astype(jnp.bfloat16)


def mul(left, right, flip=False):
    dims = (((1,), (1 if flip else 0,)), ((), ()))

    def dot(a, b):
        return lax.dot_general(a, b, dims, preferred_element_type=jnp.float32)

    both = jnp.concatenate([left[0], left[1]], axis=1)
    axis = 1 if flip else 0
    twice = jnp.concatenate([right[0], right[0]], axis=axis)
    return dot(both, twice) + dot(left[0], right[1])


def star_body(place, *refs, orders, rows):
    terms = refs[:BLOCK]
    out, tbuf, abuf, rbuf = refs[BLOCK:]
    width = out.shape[-1]
    for slot in range(BLOCK):
        origin = lax.rem(place[1] + BLOCK - slot, BLOCK)
        tbuf[lax.rem(origin + BLOCK - place[2], BLOCK)] = terms[slot][:, :width]
        abuf[origin] = terms[slot][:, width:]
    first_row = place[1] * rows if rows < width else 0
    picked = pl.ds(pl.multiple_of(first_row, 8), rows) if rows < width else pl.ds(0, rows)
    row = lax.broadcasted_iota(jnp.int32, (width, width), 0)
    col = lax.broadcasted_iota(jnp.int32, (width, width), 1)
    part_row = lax.broadcasted_iota(jnp.int32, (rows, width), 0) + first_row
    part_col = lax.broadcasted_iota(jnp.int32, (rows, width), 1)
    upper = jnp.logical_and(row < width // 2, col >= width // 2)
    lower = jnp.logical_and(row >= width // 2, col < width // 2)

    def diag(vector):
        return jnp.where(row == col, vector, 0.0)

    def part_diag(vector):
        return jnp.where(part_row == part_col, vector, 0.0)

    def steps(order):
        trans, front, back = [], [], []
        for sec in range(BLOCK):
            decay = abuf[sec, order, 0:1, :]
            mirror = abuf[sec, order, 1:2, :]
            mask = jnp.where(
                upper, abuf[sec, order, 2:3, :], jnp.where(lower, abuf[sec, order, 3:4, :], 1.0)
            )
            passing = jnp.broadcast_to(jnp.sqrt(1.0 - mirror * mirror), (width, width)).T
            trans.append(passing * (tbuf[sec, order] * mask) * decay)
            front.append(decay * decay * mirror)
            back.append(-mirror)
        yield
        bounce_a = back[0] * front[1]
        bounce_b = back[2] * front[3]
        gain_a = (1.0 + bounce_a * bounce_a) * (1.0 + bounce_a)
        gain_b = (1.0 + bounce_b * bounce_b) * (1.0 + bounce_b)
        flip_0 = trans[0].T
        flip_2 = trans[2].T
        rbuf[2 * order] = flip_0
        rbuf[2 * order + 1] = trans[3]
        flip_0_part = rbuf[2 * order, picked, :]
        trans_3_part = rbuf[2 * order + 1, picked, :]
        yield
        s0, s1, s2, s3 = [halves(t) for t in trans]
        yield
        trans_a = halves(mul(halves(trans[1] * gain_a), s0))
        yield
        back_a = halves(diag(back[1]) + mul(halves(trans[1] * (back[0] * gain_a)), s1, True))
        yield
        front_b = halves(diag(front[2]) + mul(halves(flip_2 * (front[3] * gain_b)), s2))
        yield
        trans_b = halves(mul(halves(trans[3] * gain_b), s2))
        yield
        flip_a_part = halves(mul(halves(flip_0_part * gain_a), s1, True))
        yield
        trans_b_part = mul(halves(trans_3_part * gain_b), s2)
        yield
        front_a_part = part_diag(front[0]) + mul(halves(flip_0_part * (front[1] * gain_a)), s0)
        yield
        back_b_part = part_diag(back[3]) + mul(halves(trans_3_part * (back[2] * gain_b)), s3, True)
        yield
        bounce = halves(mul(back_a, front_b))
        yield
        ahead = jnp.concatenate([trans_b_part, mul(flip_a_part, front_b)], axis=0)
        yield
        behind = mul(halves(trans_b_part), back_a)
        yield
        square = halves(mul(bounce, bounce))
        yield
        ahead = ahead + mul(halves(ahead), bounce)
        yield
        behind = behind + mul(halves(behind), bounce, True)
        yield
        ahead = ahead + mul(halves(ahead), square)
        yield
        behind = behind + mul(halves(behind), square, True)
        yield
        ahead = mul(halves(ahead), trans_a)
        out[0, order] = ahead[:rows]
        out[1, order] = front_a_part + ahead[rows:]
        yield
        out[2, order] = back_b_part + mul(halves(behind), trans_b, True)
        yield

    running = [steps(order) for order in range(orders)]
    while running:
        running = [one for one in running if next(one, 0) is None]


def star_of_four(place, terms, rows):
    orders, width = terms[0].shape[0], terms[0].shape[-1]
    extra = terms[0].shape[1] - width
    vmem = pl.BlockSpec(memory_space=pltpu.VMEM)
    return pl.pallas_call(
        functools.partial(star_body, orders=orders, rows=rows),
        out_shape=jax.ShapeDtypeStruct((3, orders, rows, width), jnp.float32),
        in_specs=[pl.BlockSpec(memory_space=pltpu.SMEM)] + [vmem] * BLOCK,
        out_specs=vmem,
        scratch_shapes=[
            pltpu.VMEM((BLOCK, orders, width, width), jnp.float32),
            pltpu.VMEM((BLOCK, orders, extra, width), jnp.float32),
            pltpu.VMEM((2 * orders, width, width), jnp.float32),
        ],
        compiler_params=ROOM,
        cost_estimate=pl.CostEstimate(
            flops=orders * 120 * width**3, bytes_accessed=orders * 8 * 4 * width**2, transcendentals=0
        ),
    )(place, *terms)


def own_body(place, pattern, decays, mirrors, *refs):
    parts, (exits, hop, out) = refs[:-3], refs[-3:]
    width = out.shape[-1]
    out[:, width:] = jnp.zeros_like(out[:, width:])
    share = out.shape[0]
    for index in range(share):
        total = parts[0][index]
        for part in parts[1:]:
            total = total + part[index]
        total = jnp.where(place[3] == 1, exits[index], total)
        out[index, :width] = jnp.where(place[3] == 2, hop[index], total)
        order = place[0] * share + index
        columns = pl.ds(pl.multiple_of(order * width, width), width)
        out[index, width : width + 1] = decays[:, columns]
        out[index, width + 1 : width + 2] = mirrors[:, columns]
        for side in (0, 1):
            flag = pattern[0, order, side].astype(jnp.float32)
            out[index, width + 2 + side : width + 3 + side] = jnp.full((1, width), flag)


def own_terms(place, pattern, decays, mirrors, parts, exits, hop):
    number, width = parts[0].shape[0], parts[0].shape[-1]
    vmem, smem = pl.BlockSpec(memory_space=pltpu.VMEM), pl.BlockSpec(memory_space=pltpu.SMEM)
    return pl.pallas_call(
        own_body,
        out_shape=jax.ShapeDtypeStruct((number, width + 8, width), jnp.float32),
        in_specs=[smem] * 2 + [vmem] * (4 + len(parts)),
        out_specs=vmem,
        compiler_params=ROOM,
        cost_estimate=pl.CostEstimate(
            flops=4 * number * width**2, bytes_accessed=28 * number * width**2, transcendentals=0
        ),
    )(place, pattern, decays, mirrors, *parts, exits, hop)


def tall_dot(left, right):
    dims = (((0,), (0,)), ((), ()))
    return lax.dot_general(left, right, dims, preferred_element_type=jnp.float32)


def hand_out(place, terms, outs):
    count = len(outs)
    for turn, out in enumerate(outs):
        out[...] = terms[lax.rem(place[0] + turn, count)]


def exit_body(place, own, after, *refs):
    outs, terms = refs[:-1], refs[-1]
    count, share, width = terms.shape[:3]
    for spot in range(count):
        for item in range(share):
            columns = pl.ds((spot * share + item) * width, width)
            terms[spot, item] = tall_dot(own[:, columns], after[:, columns])
    hand_out(place, terms, outs)


def exit_sums(place, fields, exit_modes, count, share, width):
    points, modes = fields.shape
    whole = pl.BlockSpec(memory_space=pltpu.VMEM)
    return pl.pallas_call(
        exit_body,
        out_shape=[jax.ShapeDtypeStruct((share, width, width), jnp.float32)] * count,
        in_specs=[pl.BlockSpec(memory_space=pltpu.SMEM), whole, whole],
        out_specs=[whole] * count,
        scratch_shapes=[pltpu.VMEM((count, share, width, width), jnp.float32)],
        compiler_params=ROOM,
        cost_estimate=pl.CostEstimate(
            flops=2 * points * modes * width, bytes_accessed=4 * points * modes, transcendentals=0
        ),
    )(place, fields, exit_modes)


def inner_body(place, fields, arrived, *refs):
    outs, terms = refs[:-1], refs[-1]
    count, share, width = terms.shape[:3]

    def fill(left, right):
        for order in range(count * share):
            columns = pl.ds(order * width, width)
            terms[order // share, order % share] = tall_dot(left[:, columns], right[:, columns])

    even = lax.rem(place[0], 2) == 0

    @pl.when(even)
    def _():
        fill(arrived, fields)

    @pl.when(jnp.logical_not(even))
    def _():
        fill(fields, arrived)

    hand_out(place, terms, outs)


def inner_sums(place, fields, arrived, count, share, width):
    points, modes = fields.shape
    whole = pl.BlockSpec(memory_space=pltpu.VMEM)
    return pl.pallas_call(
        inner_body,
        out_shape=[jax.ShapeDtypeStruct((share, width, width), jnp.float32)] * count,
        in_specs=[pl.BlockSpec(memory_space=pltpu.SMEM), whole, whole],
        out_specs=[whole] * count,
        scratch_shapes=[pltpu.VMEM((count, share, width, width), jnp.float32)],
        compiler_params=ROOM,
        cost_estimate=pl.CostEstimate(
            flops=2 * points * modes * width, bytes_accessed=4 * points * modes, transcendentals=0
        ),
    )(place, fields, arrived)


def body(modes, exit_modes, pattern, attenuation, reflection):
    sections, count = lax.axis_size("sec"), lax.axis_size("grid")
    sec, spot = lax.axis_index("sec"), lax.axis_index("grid")
    orders = pattern.shape[1]
    width = modes.shape[2] // orders
    share = orders // count
    fields = modes[0]
    final = sections - 1
    small = sections == BLOCK
    even = 1 - lax.rem(spot, 2)
    if small:
        late = even
        special = jnp.where(even == 1, jnp.where(sec == 0, 2, 0), jnp.where(sec == final, 1, 0))
    else:
        late = 0 * even
        special = jnp.where(sec == final, 1, 0)
    place = jnp.stack([spot, sec, late, special]).astype(jnp.int32)

    def send(value, pairs):
        return lax.ppermute(value, AXES, [(s * count + g, t * count + h) for (s, g), (t, h) in pairs])

    def gathered(parts, members):
        got = [parts[0]]
        for turn in range(1, count):
            got.append(send(parts[turn], [(row[g], row[(g + turn) % count]) for row in members for g in range(count)]))
        return got

    steps = [((s + g % 2, g), (s + 1 - g % 2, g)) for s in range(final) for g in range(count)]
    arrived = send(fields, steps)

    exit_parts = exit_sums(place, fields, exit_modes, count, share, width)
    exits = sum(gathered(exit_parts, [[(final, g) for g in range(count)]]))
    hop = send(exits, [((final, g), (0, g)) for g in range(0, count, 2)]) if small else exits

    parts = inner_sums(place, fields, arrived, count, share, width)
    parts = gathered(parts, [[(s + 1 - g % 2, g) for g in range(count)] for s in range(final)])
    if not small:
        own = sum(parts)
        back = send(own, [((s + 1, g), (s, g)) for s in range(final) for g in range(0, count, 2)])
        parts = [jnp.where(even == 1, back, own)]
    own = own_terms(place, pattern, attenuation, reflection, parts, exits, hop)
    terms = [own]
    for turn in range(1, BLOCK):
        ring = [(s, s - s % BLOCK + (s + turn) % BLOCK) for s in range(sections)]
        terms.append(send(own, [((s, g), (t, g)) for s, t in ring for g in range(count)]))
    merged = star_of_four(place, terms, width // sections if small else width)
    return merged if small else later_levels(merged, sections, sec)


def pair_body(first, second, out):
    for order in range(out.shape[1]):
        trans_a, front_a, back_a = (first[i, order] for i in range(3))
        trans_b, front_b, back_b = (second[i, order] for i in range(3))
        bounce = halves(mul(halves(back_a), halves(front_b)))
        square = halves(mul(bounce, bounce))
        inner = trans_a + mul(bounce, halves(trans_a))
        inner = halves(inner + mul(square, halves(inner)))
        behind = trans_b + mul(halves(trans_b), bounce)
        behind = halves(behind + mul(halves(behind), square))
        left = halves(trans_b)
        out[0, order] = mul(left, inner)
        out[1, order] = front_a + mul(halves(trans_a.T), halves(mul(halves(front_b), inner)))
        out[2, order] = back_b + mul(left, halves(mul(halves(back_a), behind, True)))


def later_levels(merged, sections, sec):
    vmem = pl.BlockSpec(memory_space=pltpu.VMEM)
    star = pl.pallas_call(
        pair_body, out_shape=jax.ShapeDtypeStruct(merged.shape, merged.dtype), in_specs=[vmem] * 2, out_specs=vmem
    )
    stride = BLOCK
    while stride < sections:
        other = lax.ppermute(merged, "sec", [(s, s ^ stride) for s in range(sections)])
        high = lax.rem(lax.div(sec, stride), 2) == 1
        merged = star(jnp.where(high, other, merged), jnp.where(high, merged, other))
        stride *= 2
    rows = merged.shape[2] // sections
    return lax.dynamic_slice_in_dim(merged, sec * rows, rows, 2)


def solution(mesh):
    in_specs = (
        P(("groups", "sec"), "grid", None),
        P(("groups", "grid"), None),
        P(("groups", "sec"), None, None),
        P(("groups", "sec"), None),
        P(("groups", "sec"), None),
    )
    out_specs = P("groups", "grid", "sec", None)
    return jax.shard_map(body, mesh=mesh, in_specs=in_specs, out_specs=out_specs, check_vma=False)
```

```python
import functools

import jax
import jax.numpy as jnp
from jax import lax
from jax.experimental import pallas as pl
from jax.experimental.pallas import tpu as pltpu
from jax.sharding import PartitionSpec as P

BLOCK = 4
AXES = ("sec", "grid")
ROOM = pltpu.CompilerParams(vmem_limit_bytes=16 * 2**20)


def halves(matrix):
    high = matrix.astype(jnp.bfloat16)
    return high, (matrix - high.astype(jnp.float32)).astype(jnp.bfloat16)


def mul(left, right, flip=False):
    dims = (((1,), (1 if flip else 0,)), ((), ()))

    def dot(a, b):
        return lax.dot_general(a, b, dims, preferred_element_type=jnp.float32)

    both = jnp.concatenate([left[0], left[1]], axis=1)
    axis = 1 if flip else 0
    twice = jnp.concatenate([right[0], right[0]], axis=axis)
    return dot(both, twice) + dot(left[0], right[1])


def star_body(place, *refs, orders, rows):
    terms = refs[:BLOCK]
    out, tbuf, abuf, rbuf = refs[BLOCK:]
    width = out.shape[-1]
    for slot in range(BLOCK):
        origin = lax.rem(place[1] + BLOCK - slot, BLOCK)
        tbuf[lax.rem(origin + BLOCK - place[2], BLOCK)] = terms[slot][:, :width]
        abuf[origin] = terms[slot][:, width:]
    first_row = place[1] * rows if rows < width else 0
    picked = pl.ds(pl.multiple_of(first_row, 8), rows) if rows < width else pl.ds(0, rows)
    row = lax.broadcasted_iota(jnp.int32, (width, width), 0)
    col = lax.broadcasted_iota(jnp.int32, (width, width), 1)
    part_row = lax.broadcasted_iota(jnp.int32, (rows, width), 0) + first_row
    part_col = lax.broadcasted_iota(jnp.int32, (rows, width), 1)
    upper = jnp.logical_and(row < width // 2, col >= width // 2)
    lower = jnp.logical_and(row >= width // 2, col < width // 2)

    def diag(vector):
        return jnp.where(row == col, vector, 0.0)

    def part_diag(vector):
        return jnp.where(part_row == part_col, vector, 0.0)

    def steps(order):
        trans, front, back = [], [], []
        for sec in range(BLOCK):
            decay = abuf[sec, order, 0:1, :]
            mirror = abuf[sec, order, 1:2, :]
            mask = jnp.where(
                upper, abuf[sec, order, 2:3, :], jnp.where(lower, abuf[sec, order, 3:4, :], 1.0)
            )
            passing = jnp.broadcast_to(jnp.sqrt(1.0 - mirror * mirror), (width, width)).T
            trans.append(passing * (tbuf[sec, order] * mask) * decay)
            front.append(decay * decay * mirror)
            back.append(-mirror)
        yield
        bounce_a = back[0] * front[1]
        bounce_b = back[2] * front[3]
        gain_a = (1.0 + bounce_a * bounce_a) * (1.0 + bounce_a)
        gain_b = (1.0 + bounce_b * bounce_b) * (1.0 + bounce_b)
        flip_0 = trans[0].T
        flip_2 = trans[2].T
        rbuf[2 * order] = flip_0
        rbuf[2 * order + 1] = trans[3]
        flip_0_part = rbuf[2 * order, picked, :]
        trans_3_part = rbuf[2 * order + 1, picked, :]
        yield
        s0, s1, s2, s3 = [halves(t) for t in trans]
        yield
        trans_a = halves(mul(halves(trans[1] * gain_a), s0))
        yield
        back_a = halves(diag(back[1]) + mul(halves(trans[1] * (back[0] * gain_a)), s1, True))
        yield
        front_b = halves(diag(front[2]) + mul(halves(flip_2 * (front[3] * gain_b)), s2))
        yield
        trans_b = halves(mul(halves(trans[3] * gain_b), s2))
        yield
        flip_a_part = halves(mul(halves(flip_0_part * gain_a), s1, True))
        yield
        trans_b_part = mul(halves(trans_3_part * gain_b), s2)
        yield
        front_a_part = part_diag(front[0]) + mul(halves(flip_0_part * (front[1] * gain_a)), s0)
        yield
        back_b_part = part_diag(back[3]) + mul(halves(trans_3_part * (back[2] * gain_b)), s3, True)
        yield
        bounce = halves(mul(back_a, front_b))
        yield
        ahead = jnp.concatenate([trans_b_part, mul(flip_a_part, front_b)], axis=0)
        yield
        behind = mul(halves(trans_b_part), back_a)
        yield
        square = halves(mul(bounce, bounce))
        yield
        ahead = ahead + mul(halves(ahead), bounce)
        yield
        behind = behind + mul(halves(behind), bounce, True)
        yield
        ahead = ahead + mul(halves(ahead), square)
        yield
        behind = behind + mul(halves(behind), square, True)
        yield
        ahead = mul(halves(ahead), trans_a)
        out[0, order] = ahead[:rows]
        out[1, order] = front_a_part + ahead[rows:]
        yield
        out[2, order] = back_b_part + mul(halves(behind), trans_b, True)
        yield

    running = [steps(order) for order in range(orders)]
    while running:
        running = [one for one in running if next(one, 0) is None]


def star_of_four(place, terms, rows):
    orders, width = terms[0].shape[0], terms[0].shape[-1]
    extra = terms[0].shape[1] - width
    vmem = pl.BlockSpec(memory_space=pltpu.VMEM)
    return pl.pallas_call(
        functools.partial(star_body, orders=orders, rows=rows),
        out_shape=jax.ShapeDtypeStruct((3, orders, rows, width), jnp.float32),
        in_specs=[pl.BlockSpec(memory_space=pltpu.SMEM)] + [vmem] * BLOCK,
        out_specs=vmem,
        scratch_shapes=[
            pltpu.VMEM((BLOCK, orders, width, width), jnp.float32),
            pltpu.VMEM((BLOCK, orders, extra, width), jnp.float32),
            pltpu.VMEM((2 * orders, width, width), jnp.float32),
        ],
        compiler_params=ROOM,
        cost_estimate=pl.CostEstimate(
            flops=orders * 120 * width**3, bytes_accessed=orders * 8 * 4 * width**2, transcendentals=0
        ),
    )(place, *terms)


def own_body(place, pattern, decays, mirrors, *refs):
    parts, (exits, hop, out) = refs[:-3], refs[-3:]
    width = out.shape[-1]
    out[:, width:] = jnp.zeros_like(out[:, width:])
    share = out.shape[0]
    for index in range(share):
        total = parts[0][index]
        for part in parts[1:]:
            total = total + part[index]
        total = jnp.where(place[3] == 1, exits[index], total)
        out[index, :width] = jnp.where(place[3] == 2, hop[index], total)
        order = place[0] * share + index
        columns = pl.ds(pl.multiple_of(order * width, width), width)
        out[index, width : width + 1] = decays[:, columns]
        out[index, width + 1 : width + 2] = mirrors[:, columns]
        for side in (0, 1):
            flag = pattern[0, order, side].astype(jnp.float32)
            out[index, width + 2 + side : width + 3 + side] = jnp.full((1, width), flag)


def own_terms(place, pattern, decays, mirrors, parts, exits, hop):
    number, width = parts[0].shape[0], parts[0].shape[-1]
    vmem, smem = pl.BlockSpec(memory_space=pltpu.VMEM), pl.BlockSpec(memory_space=pltpu.SMEM)
    return pl.pallas_call(
        own_body,
        out_shape=jax.ShapeDtypeStruct((number, width + 8, width), jnp.float32),
        in_specs=[smem] * 2 + [vmem] * (4 + len(parts)),
        out_specs=vmem,
        compiler_params=ROOM,
        cost_estimate=pl.CostEstimate(
            flops=4 * number * width**2, bytes_accessed=28 * number * width**2, transcendentals=0
        ),
    )(place, pattern, decays, mirrors, *parts, exits, hop)


def tall_dot(left, right):
    dims = (((0,), (0,)), ((), ()))
    return lax.dot_general(left, right, dims, preferred_element_type=jnp.float32)


def hand_out(place, terms, outs):
    count = len(outs)
    for turn, out in enumerate(outs):
        out[...] = terms[lax.rem(place[0] + turn, count)]


def exit_body(place, own, after, *refs):
    outs, terms = refs[:-1], refs[-1]
    count, share, width = terms.shape[:3]
    for spot in range(count):
        for item in range(share):
            columns = pl.ds((spot * share + item) * width, width)
            terms[spot, item] = tall_dot(own[:, columns], after[:, columns])
    hand_out(place, terms, outs)


def exit_sums(place, fields, exit_modes, count, share, width):
    points, modes = fields.shape
    whole = pl.BlockSpec(memory_space=pltpu.VMEM)
    return pl.pallas_call(
        exit_body,
        out_shape=[jax.ShapeDtypeStruct((share, width, width), jnp.float32)] * count,
        in_specs=[pl.BlockSpec(memory_space=pltpu.SMEM), whole, whole],
        out_specs=[whole] * count,
        scratch_shapes=[pltpu.VMEM((count, share, width, width), jnp.float32)],
        compiler_params=ROOM,
        cost_estimate=pl.CostEstimate(
            flops=2 * points * modes * width, bytes_accessed=4 * points * modes, transcendentals=0
        ),
    )(place, fields, exit_modes)


def pack_body(place, fields, mine, sibling, *, pairs):
    parity = lax.rem(place[0], 2)
    size = mine.shape[1] // pairs
    for pair in range(pairs):
        target = pl.ds(pair * size, size)
        mine[:, target] = fields[:, pl.ds(pl.multiple_of((2 * pair + parity) * size, 128), size)]
        sibling[:, target] = fields[:, pl.ds(pl.multiple_of((2 * pair + 1 - parity) * size, 128), size)]


def packed(place, fields, pairs):
    points, modes = fields.shape
    vmem = pl.BlockSpec(memory_space=pltpu.VMEM)
    return pl.pallas_call(
        functools.partial(pack_body, pairs=pairs),
        out_shape=[jax.ShapeDtypeStruct((points, modes // 2), fields.dtype)] * 2,
        in_specs=[pl.BlockSpec(memory_space=pltpu.SMEM), vmem],
        out_specs=[vmem] * 2,
        compiler_params=ROOM,
        cost_estimate=pl.CostEstimate(flops=0, bytes_accessed=4 * points * modes, transcendentals=0),
    )(place, fields)


def inner_body(place, *refs, pairs):
    own, arrived, outs, terms = refs[:2], refs[2:4], refs[4:-1], refs[-1]
    share, width = terms.shape[1], terms.shape[-1]

    def fill(left, right):
        for order in range(pairs * share):
            columns = pl.ds(order * width, width)
            terms[order // share, order % share] = tall_dot(left[0][:, columns], right[0][:, columns]) + tall_dot(
                left[1][:, columns], right[1][:, columns]
            )

    even = lax.rem(place[0], 2) == 0

    @pl.when(even)
    def _():
        fill(arrived, own)

    @pl.when(jnp.logical_not(even))
    def _():
        fill(own, arrived)

    for turn, out in enumerate(outs):
        out[...] = terms[lax.rem(lax.div(place[0], 2) + turn, pairs)]


def inner_sums(place, own, arrived, pairs, share, width):
    points = own[0].shape[0]
    whole = pl.BlockSpec(memory_space=pltpu.VMEM)
    return pl.pallas_call(
        functools.partial(inner_body, pairs=pairs),
        out_shape=[jax.ShapeDtypeStruct((share, width, width), jnp.float32)] * pairs,
        in_specs=[pl.BlockSpec(memory_space=pltpu.SMEM)] + [whole] * 4,
        out_specs=[whole] * pairs,
        scratch_shapes=[pltpu.VMEM((pairs, share, width, width), jnp.float32)],
        compiler_params=ROOM,
        cost_estimate=pl.CostEstimate(
            flops=4 * points * pairs * share * width**2,
            bytes_accessed=8 * points * pairs * share * width,
            transcendentals=0,
        ),
    )(place, *own, *arrived)


def body(modes, exit_modes, pattern, attenuation, reflection):
    sections, count = lax.axis_size("sec"), lax.axis_size("grid")
    sec, spot = lax.axis_index("sec"), lax.axis_index("grid")
    orders = pattern.shape[1]
    width = modes.shape[2] // orders
    share = orders // count
    fields = modes[0]
    final = sections - 1
    small = sections == BLOCK
    even = 1 - lax.rem(spot, 2)
    if small:
        late = even
        special = jnp.where(even == 1, jnp.where(sec == 0, 2, 0), jnp.where(sec == final, 1, 0))
    else:
        late = 0 * even
        special = jnp.where(sec == final, 1, 0)
    place = jnp.stack([spot, sec, late, special]).astype(jnp.int32)

    def send(value, pairs):
        return lax.ppermute(value, AXES, [(s * count + g, t * count + h) for (s, g), (t, h) in pairs])

    def gathered(parts, members):
        got = [parts[0]]
        for turn in range(1, count):
            got.append(send(parts[turn], [(row[g], row[(g + turn) % count]) for row in members for g in range(count)]))
        return got

    pairs = count // 2
    mine, sibling = packed(place, fields, pairs)
    steps = [((s + g % 2, g), (s + 1 - g % 2, g)) for s in range(final) for g in range(count)]
    beside = send(sibling, [((s, g), (s, g ^ 1)) for s in range(sections) for g in range(count)])
    own_fields = (mine, beside)
    arrived = (send(mine, steps), send(beside, steps))

    exit_parts = exit_sums(place, fields, exit_modes, count, share, width)
    exits = sum(gathered(exit_parts, [[(final, g) for g in range(count)]]))
    hop = send(exits, [((final, g), (0, g)) for g in range(0, count, 2)]) if small else exits

    parts = list(inner_sums(place, own_fields, arrived, pairs, share, width))
    for turn in range(1, pairs):
        ring = [((s, g), (s, (g + 2 * turn) % count)) for s in range(sections) for g in range(count)]
        parts[turn] = send(parts[turn], ring)
    if not small:
        own = sum(parts)
        back = send(own, [((s + 1, g), (s, g)) for s in range(final) for g in range(0, count, 2)])
        parts = [jnp.where(even == 1, back, own)]
    own = own_terms(place, pattern, attenuation, reflection, parts, exits, hop)
    terms = [own]
    for turn in range(1, BLOCK):
        ring = [(s, s - s % BLOCK + (s + turn) % BLOCK) for s in range(sections)]
        terms.append(send(own, [((s, g), (t, g)) for s, t in ring for g in range(count)]))
    merged = star_of_four(place, terms, width // sections if small else width)
    return merged if small else later_levels(merged, sections, sec)


def pair_body(first, second, out):
    for order in range(out.shape[1]):
        trans_a, front_a, back_a = (first[i, order] for i in range(3))
        trans_b, front_b, back_b = (second[i, order] for i in range(3))
        bounce = halves(mul(halves(back_a), halves(front_b)))
        square = halves(mul(bounce, bounce))
        inner = trans_a + mul(bounce, halves(trans_a))
        inner = halves(inner + mul(square, halves(inner)))
        behind = trans_b + mul(halves(trans_b), bounce)
        behind = halves(behind + mul(halves(behind), square))
        left = halves(trans_b)
        out[0, order] = mul(left, inner)
        out[1, order] = front_a + mul(halves(trans_a.T), halves(mul(halves(front_b), inner)))
        out[2, order] = back_b + mul(left, halves(mul(halves(back_a), behind, True)))


def later_levels(merged, sections, sec):
    vmem = pl.BlockSpec(memory_space=pltpu.VMEM)
    star = pl.pallas_call(
        pair_body, out_shape=jax.ShapeDtypeStruct(merged.shape, merged.dtype), in_specs=[vmem] * 2, out_specs=vmem
    )
    stride = BLOCK
    while stride < sections:
        other = lax.ppermute(merged, "sec", [(s, s ^ stride) for s in range(sections)])
        high = lax.rem(lax.div(sec, stride), 2) == 1
        merged = star(jnp.where(high, other, merged), jnp.where(high, merged, other))
        stride *= 2
    rows = merged.shape[2] // sections
    return lax.dynamic_slice_in_dim(merged, sec * rows, rows, 2)


def solution(mesh):
    in_specs = (
        P(("groups", "sec"), "grid", None),
        P(("groups", "grid"), None),
        P(("groups", "sec"), None, None),
        P(("groups", "sec"), None),
        P(("groups", "sec"), None),
    )
    out_specs = P("groups", "grid", "sec", None)
    return jax.shard_map(body, mesh=mesh, in_specs=in_specs, out_specs=out_specs, check_vma=False)
```

```python
import functools

import jax
import jax.numpy as jnp
from jax import lax
from jax.experimental import pallas as pl
from jax.experimental.pallas import tpu as pltpu
from jax.sharding import PartitionSpec as P

BLOCK = 4
AXES = ("sec", "grid")
ROOM = pltpu.CompilerParams(vmem_limit_bytes=16 * 2**20)


def halves(matrix):
    high = matrix.astype(jnp.bfloat16)
    return high, (matrix - high.astype(jnp.float32)).astype(jnp.bfloat16)


def mul(left, right, flip=False):
    dims = (((1,), (1 if flip else 0,)), ((), ()))

    def dot(a, b):
        return lax.dot_general(a, b, dims, preferred_element_type=jnp.float32)

    both = jnp.concatenate([left[0], left[1]], axis=1)
    axis = 1 if flip else 0
    twice = jnp.concatenate([right[0], right[0]], axis=axis)
    return dot(both, twice) + dot(left[0], right[1])


def star_body(place, *refs, orders, rows):
    terms, done = refs[:BLOCK], refs[BLOCK:-4]
    out, tbuf, abuf, rbuf = refs[-4:]
    earlier = out.shape[1] - orders
    for ready in done:
        out[:, :earlier] = ready[...]
    width = out.shape[-1]
    for slot in range(BLOCK):
        origin = lax.rem(place[1] + BLOCK - slot, BLOCK)
        tbuf[lax.rem(origin + BLOCK - place[2], BLOCK)] = terms[slot][:, :width]
        abuf[origin] = terms[slot][:, width:]
    first_row = place[1] * rows if rows < width else 0
    picked = pl.ds(pl.multiple_of(first_row, 8), rows) if rows < width else pl.ds(0, rows)
    row = lax.broadcasted_iota(jnp.int32, (width, width), 0)
    col = lax.broadcasted_iota(jnp.int32, (width, width), 1)
    part_row = lax.broadcasted_iota(jnp.int32, (rows, width), 0) + first_row
    part_col = lax.broadcasted_iota(jnp.int32, (rows, width), 1)
    upper = jnp.logical_and(row < width // 2, col >= width // 2)
    lower = jnp.logical_and(row >= width // 2, col < width // 2)

    def diag(vector):
        return jnp.where(row == col, vector, 0.0)

    def part_diag(vector):
        return jnp.where(part_row == part_col, vector, 0.0)

    def steps(order):
        trans, front, back = [], [], []
        for sec in range(BLOCK):
            decay = abuf[sec, order, 0:1, :]
            mirror = abuf[sec, order, 1:2, :]
            mask = jnp.where(
                upper, abuf[sec, order, 2:3, :], jnp.where(lower, abuf[sec, order, 3:4, :], 1.0)
            )
            passing = jnp.broadcast_to(jnp.sqrt(1.0 - mirror * mirror), (width, width)).T
            trans.append(passing * (tbuf[sec, order] * mask) * decay)
            front.append(decay * decay * mirror)
            back.append(-mirror)
        yield
        bounce_a = back[0] * front[1]
        bounce_b = back[2] * front[3]
        gain_a = (1.0 + bounce_a * bounce_a) * (1.0 + bounce_a)
        gain_b = (1.0 + bounce_b * bounce_b) * (1.0 + bounce_b)
        flip_0 = trans[0].T
        flip_2 = trans[2].T
        rbuf[2 * order] = flip_0
        rbuf[2 * order + 1] = trans[3]
        flip_0_part = rbuf[2 * order, picked, :]
        trans_3_part = rbuf[2 * order + 1, picked, :]
        yield
        s0, s1, s2, s3 = [halves(t) for t in trans]
        yield
        trans_a = halves(mul(halves(trans[1] * gain_a), s0))
        yield
        back_a = halves(diag(back[1]) + mul(halves(trans[1] * (back[0] * gain_a)), s1, True))
        yield
        front_b = halves(diag(front[2]) + mul(halves(flip_2 * (front[3] * gain_b)), s2))
        yield
        trans_b = halves(mul(halves(trans[3] * gain_b), s2))
        yield
        flip_a_part = halves(mul(halves(flip_0_part * gain_a), s1, True))
        yield
        trans_b_part = mul(halves(trans_3_part * gain_b), s2)
        yield
        front_a_part = part_diag(front[0]) + mul(halves(flip_0_part * (front[1] * gain_a)), s0)
        yield
        back_b_part = part_diag(back[3]) + mul(halves(trans_3_part * (back[2] * gain_b)), s3, True)
        yield
        bounce = halves(mul(back_a, front_b))
        yield
        ahead = jnp.concatenate([trans_b_part, mul(flip_a_part, front_b)], axis=0)
        yield
        behind = mul(halves(trans_b_part), back_a)
        yield
        square = halves(mul(bounce, bounce))
        yield
        ahead = ahead + mul(halves(ahead), bounce)
        yield
        behind = behind + mul(halves(behind), bounce, True)
        yield
        ahead = ahead + mul(halves(ahead), square)
        yield
        behind = behind + mul(halves(behind), square, True)
        yield
        ahead = mul(halves(ahead), trans_a)
        out[0, earlier + order] = ahead[:rows]
        out[1, earlier + order] = front_a_part + ahead[rows:]
        yield
        out[2, earlier + order] = back_b_part + mul(halves(behind), trans_b, True)
        yield

    running = [steps(order) for order in range(orders)]
    while running:
        running = [one for one in running if next(one, 0) is None]


def star_of_four(place, terms, rows, done):
    orders, width = terms[0].shape[0], terms[0].shape[-1]
    extra = terms[0].shape[1] - width
    earlier = sum(ready.shape[1] for ready in done)
    vmem = pl.BlockSpec(memory_space=pltpu.VMEM)
    return pl.pallas_call(
        functools.partial(star_body, orders=orders, rows=rows),
        out_shape=jax.ShapeDtypeStruct((3, earlier + orders, rows, width), jnp.float32),
        in_specs=[pl.BlockSpec(memory_space=pltpu.SMEM)] + [vmem] * (BLOCK + len(done)),
        out_specs=vmem,
        scratch_shapes=[
            pltpu.VMEM((BLOCK, orders, width, width), jnp.float32),
            pltpu.VMEM((BLOCK, orders, extra, width), jnp.float32),
            pltpu.VMEM((2 * orders, width, width), jnp.float32),
        ],
        compiler_params=ROOM,
        cost_estimate=pl.CostEstimate(
            flops=orders * 120 * width**3, bytes_accessed=orders * 8 * 4 * width**2, transcendentals=0
        ),
    )(place, *terms, *done)


def own_body(place, pattern, decays, mirrors, *refs, item):
    parts, (exits, hop, out) = refs[:-3], refs[-3:]
    width = out.shape[-1]
    out[:, width:] = jnp.zeros_like(out[:, width:])
    share = exits.shape[0]
    total = parts[0][0]
    for part in parts[1:]:
        total = total + part[0]
    total = jnp.where(place[3] == 1, exits[item], total)
    out[0, :width] = jnp.where(place[3] == 2, hop[item], total)
    order = place[0] * share + item
    columns = pl.ds(pl.multiple_of(order * width, width), width)
    out[0, width : width + 1] = decays[:, columns]
    out[0, width + 1 : width + 2] = mirrors[:, columns]
    for side in (0, 1):
        flag = pattern[0, order, side].astype(jnp.float32)
        out[0, width + 2 + side : width + 3 + side] = jnp.full((1, width), flag)


def own_terms(place, pattern, decays, mirrors, parts, exits, hop, item):
    number, width = parts[0].shape[0], parts[0].shape[-1]
    vmem, smem = pl.BlockSpec(memory_space=pltpu.VMEM), pl.BlockSpec(memory_space=pltpu.SMEM)
    return pl.pallas_call(
        functools.partial(own_body, item=item),
        out_shape=jax.ShapeDtypeStruct((number, width + 8, width), jnp.float32),
        in_specs=[smem] * 2 + [vmem] * (4 + len(parts)),
        out_specs=vmem,
        compiler_params=ROOM,
        cost_estimate=pl.CostEstimate(
            flops=4 * number * width**2, bytes_accessed=28 * number * width**2, transcendentals=0
        ),
    )(place, pattern, decays, mirrors, *parts, exits, hop)


def tall_dot(left, right):
    dims = (((0,), (0,)), ((), ()))
    return lax.dot_general(left, right, dims, preferred_element_type=jnp.float32)


def pack_body(place, fields, *outs, pairs):
    share, width = len(outs) // 2, outs[0].shape[1] // pairs
    parity = lax.rem(place[0], 2)
    for index, out in enumerate(outs):
        kind = parity if index % 2 == 0 else 1 - parity
        for pair in range(pairs):
            order = (2 * pair + kind) * share + index // 2
            out[:, pl.ds(pair * width, width)] = fields[:, pl.ds(pl.multiple_of(order * width, width), width)]


def packed(place, fields, pairs, share):
    points, modes = fields.shape
    vmem = pl.BlockSpec(memory_space=pltpu.VMEM)
    return pl.pallas_call(
        functools.partial(pack_body, pairs=pairs),
        out_shape=[jax.ShapeDtypeStruct((points, modes // (2 * share)), fields.dtype)] * (2 * share),
        in_specs=[pl.BlockSpec(memory_space=pltpu.SMEM), vmem],
        out_specs=[vmem] * (2 * share),
        compiler_params=ROOM,
        cost_estimate=pl.CostEstimate(flops=0, bytes_accessed=4 * points * modes, transcendentals=0),
    )(place, fields)


def inner_body(place, *refs, pairs, ends):
    outs, terms = refs[-1 - pairs : -1], refs[-1]
    items, width = terms.shape[1], terms.shape[-1]
    own, arrived = refs[: 2 * items], refs[2 * items : 4 * items]

    def fill(left, right):
        for pair in range(pairs):
            for item in range(items):
                columns = pl.ds(pair * width, width)
                blocks = range(2 * item, 2 * item + 2)
                first, second = [tall_dot(left[i][:, columns], right[i][:, columns]) for i in blocks]
                terms[pair, item] = first + second

    if ends:
        fill(own, arrived)
    else:
        even = lax.rem(place[0], 2) == 0

        @pl.when(even)
        def _():
            fill(arrived, own)

        @pl.when(jnp.logical_not(even))
        def _():
            fill(own, arrived)

    for turn, out in enumerate(outs):
        out[...] = terms[lax.rem(lax.div(place[0], 2) + turn, pairs)]


def inner_sums(place, own, arrived, pairs, width, ends=False):
    points, items = own[0].shape[0], len(own) // 2
    whole = pl.BlockSpec(memory_space=pltpu.VMEM)
    return pl.pallas_call(
        functools.partial(inner_body, pairs=pairs, ends=ends),
        out_shape=[jax.ShapeDtypeStruct((items, width, width), jnp.float32)] * pairs,
        in_specs=[pl.BlockSpec(memory_space=pltpu.SMEM)] + [whole] * (4 * items),
        out_specs=[whole] * pairs,
        scratch_shapes=[pltpu.VMEM((pairs, items, width, width), jnp.float32)],
        compiler_params=ROOM,
        cost_estimate=pl.CostEstimate(
            flops=4 * points * pairs * items * width**2,
            bytes_accessed=8 * points * pairs * items * width,
            transcendentals=0,
        ),
    )(place, *own, *arrived)


def body(modes, exit_modes, pattern, attenuation, reflection):
    sections, count = lax.axis_size("sec"), lax.axis_size("grid")
    sec, spot = lax.axis_index("sec"), lax.axis_index("grid")
    orders = pattern.shape[1]
    width = modes.shape[2] // orders
    share = orders // count
    fields = modes[0]
    final = sections - 1
    small = sections == BLOCK
    even = 1 - lax.rem(spot, 2)
    if small:
        late = even
        special = jnp.where(even == 1, jnp.where(sec == 0, 2, 0), jnp.where(sec == final, 1, 0))
    else:
        late = 0 * even
        special = jnp.where(sec == final, 1, 0)
    place = jnp.stack([spot, sec, late, special]).astype(jnp.int32)

    def send(value, pairs):
        return lax.ppermute(value, AXES, [(s * count + g, t * count + h) for (s, g), (t, h) in pairs])

    grid, pairs = range(count), count // 2
    everywhere = [(s, g) for s in range(sections) for g in grid]

    def beside(columns):
        got = [send(columns[2 * item + 1], [((s, g), (s, g ^ 1)) for s, g in everywhere]) for item in range(share)]
        return [[columns[2 * item], got[item]] for item in range(share)]

    def summed_over(parts, members):
        got = [parts[0]]
        for turn in range(1, pairs):
            got.append(send(parts[turn], [((s, g), (s, (g + 2 * turn) % count)) for s, g in members]))
        return got

    steps = [((s + g % 2, g), (s + 1 - g % 2, g)) for s in range(final) for g in grid]
    own_fields = beside(packed(place, fields, pairs, share))
    arrived = [[send(block, steps) for block in blocks] for blocks in own_fields]

    ending = beside(packed(place, exit_modes, pairs, share))
    exit_parts = inner_sums(place, sum(own_fields, []), sum(ending, []), pairs, width, True)
    exits = sum(summed_over(exit_parts, [(final, g) for g in grid]))
    hop = send(exits, [((final, g), (0, g)) for g in grid if g % 2 == 0]) if small else exits

    done = []
    for item in range(share):
        parts = inner_sums(place, own_fields[item], arrived[item], pairs, width)
        parts = summed_over(parts, everywhere)
        if not small:
            own = sum(parts)
            back = send(own, [((s + 1, g), (s, g)) for s in range(final) for g in grid if g % 2 == 0])
            parts = [jnp.where(even == 1, back, own)]
        own = own_terms(place, pattern, attenuation, reflection, parts, exits, hop, item)
        terms = [own]
        for turn in range(1, BLOCK):
            ring = [(s, s - s % BLOCK + (s + turn) % BLOCK) for s in range(sections)]
            terms.append(send(own, [((s, g), (t, g)) for s, t in ring for g in grid]))
        done = [star_of_four(place, terms, width // sections if small else width, done)]
    return done[0] if small else later_levels(done[0], sections, sec)


def pair_body(first, second, out):
    for order in range(out.shape[1]):
        trans_a, front_a, back_a = (first[i, order] for i in range(3))
        trans_b, front_b, back_b = (second[i, order] for i in range(3))
        bounce = halves(mul(halves(back_a), halves(front_b)))
        square = halves(mul(bounce, bounce))
        inner = trans_a + mul(bounce, halves(trans_a))
        inner = halves(inner + mul(square, halves(inner)))
        behind = trans_b + mul(halves(trans_b), bounce)
        behind = halves(behind + mul(halves(behind), square))
        left = halves(trans_b)
        out[0, order] = mul(left, inner)
        out[1, order] = front_a + mul(halves(trans_a.T), halves(mul(halves(front_b), inner)))
        out[2, order] = back_b + mul(left, halves(mul(halves(back_a), behind, True)))


def later_levels(merged, sections, sec):
    vmem = pl.BlockSpec(memory_space=pltpu.VMEM)
    star = pl.pallas_call(
        pair_body, out_shape=jax.ShapeDtypeStruct(merged.shape, merged.dtype), in_specs=[vmem] * 2, out_specs=vmem
    )
    stride = BLOCK
    while stride < sections:
        other = lax.ppermute(merged, "sec", [(s, s ^ stride) for s in range(sections)])
        high = lax.rem(lax.div(sec, stride), 2) == 1
        merged = star(jnp.where(high, other, merged), jnp.where(high, merged, other))
        stride *= 2
    rows = merged.shape[2] // sections
    return lax.dynamic_slice_in_dim(merged, sec * rows, rows, 2)


def solution(mesh):
    in_specs = (
        P(("groups", "sec"), "grid", None),
        P(("groups", "grid"), None),
        P(("groups", "sec"), None, None),
        P(("groups", "sec"), None),
        P(("groups", "sec"), None),
    )
    out_specs = P("groups", "grid", "sec", None)
    return jax.shard_map(body, mesh=mesh, in_specs=in_specs, out_specs=out_specs, check_vma=False)
```
